256 devices in a mesh: row: 16 (over x_hi, z), col: 16 (over y, x_lo, core).
Axes of the slice: x: 4 (x_hi: 2, x_lo: 2; x = x_hi * 2 + x_lo), y: 4, z: 8, core: 2. Of those that a mesh axis runs over, the one named last changes fastest.
Arguments:
- panel: bfloat16 [1536, 147456], P('col', 'row'), may hold values from -3 to 3
- eigenvalues: float32 [1536], P('col'), may hold values from 0.3 to 3
- positions: float32 [3, 49152], P(None, 'row'), may hold values from -6 to 6
- elements: int32 [49152], P('row'), may hold values from 0 to 4
- radii: float32 [5], replicated, may hold values from 0.5 to 2
- neighbors: int32 [384, 5], P('row'), may hold values from 0 to 383, as said below
Outputs:
- forces: float32 [3, 49152], P(None, ('row', 'col'))
The draws below stay inside these ranges and needn't reach their ends.
Inputs may be any that keep to these rules, and one draw needn't show every extreme that they name: neighbors[I, k] lies within 24 tiles of I; slot 0 holds I + 24 and slot 1 holds I - 24, each clamped to the tiles that exist; the others are distinct offsets within that reach, clamped.
All inputs are finite; a program needn't handle non-finite values.
Results may differ from the reference program's by a relative error of at most 0.0029.
Values may be sent and summed in bfloat16 or wider, within the bound.
No kernel may reach another device: no remote copies, remote signals or barrier semaphores. Data moves between devices by JAX's collectives and lax.ppermute only.
A program may use at most 64 MiB of HBM per device.

```python
import math
import jax
import jax.numpy as jnp
from jax import lax

P_SIZE = 1536
BLK = 128
NEIGH = 5
NTYPES = 5
ATOM_DEV = 3072
NATOMS = 49152


def draw_neighbors(key, part):
    key = jax.random.fold_in(key, 7)
    count_tiles = NATOMS // BLK
    reach = ATOM_DEV // BLK
    window = 2 * reach + 1
    scores = jax.random.randint(key, (count_tiles, window), 0, 1 << 20) * window + jnp.arange(window, dtype=jnp.int32)[None, :]
    picked = jnp.argsort(scores, axis=1)[:, :NEIGH - 2].astype(jnp.int32) - reach
    upper = jnp.full((count_tiles, 1), reach, jnp.int32)
    offsets = jnp.concatenate([upper, -upper, picked], axis=1)
    tiles = jnp.arange(count_tiles, dtype=jnp.int32)[:, None] + offsets
    return jnp.clip(tiles, 0, count_tiles - 1).astype(jnp.int32)


def touch_ends(array, key, smallest, largest):
    shape = array.shape
    place = [jax.random.randint(jax.random.fold_in(key, axis), (), 0, shape[axis]) for axis in range(len(shape))]
    array = array.at[tuple(place)].set(smallest)
    longest = shape.index(max(shape))
    place[longest] = (place[longest] + 1) % shape[longest]
    return array.at[tuple(place)].set(largest)


def steps_of(key, dims, split, low, top_value):
    gain, own = 1.0, jax.random.fold_in(key, 6)
    for dim, parts in split:
        heights = jnp.exp(jax.random.uniform(jax.random.fold_in(own, dim), (parts,), jnp.float32, low / len(split), top_value / len(split)))
        gain = gain * jnp.repeat(heights, dims[dim] // parts).reshape([-1 if axis == dim else 1 for axis in range(len(dims))])
    return gain


def gaussian(own_key, shape, deviation, bound, cuts=(), kind=jnp.bfloat16):
    values = jax.random.normal(own_key, shape, jnp.float32) * deviation
    if len(cuts) > 0:
        values = steps_of(own_key, shape, cuts, -0.22, 0.18) * values
    return jnp.clip(values, min=-bound, max=bound).astype(kind)


def setup_inputs(seed: int = 0) -> dict:
    streams_of = jax.random.split(jax.random.key(seed), 7)
    panel = gaussian(streams_of[0], (P_SIZE, 3 * NATOMS), 0.2, 3.0, ((0, 16), (1, 16)))
    eigenvalues = jnp.clip(jnp.exp(math.log(3.0) - 2.3025851 * jax.random.uniform(streams_of[1], (P_SIZE,), jnp.float32) ** steps_of(streams_of[1], (P_SIZE,), ((0, 16),), -0.2, 0.2)), 0.3, 3.0)
    positions = gaussian(streams_of[2], (3, NATOMS), 1.0, 6.0, ((1, 16),), jnp.float32)
    elements = touch_ends(jax.random.randint(streams_of[3], (NATOMS,), 0, NTYPES), jax.random.fold_in(streams_of[3], 1), 0, NTYPES - 1).astype(jnp.int32)
    radii = jnp.clip(jax.random.uniform(streams_of[4], (NTYPES,), jnp.float32, 0.5, 2.0), 0.5, 2.0)
    neighbors = draw_neighbors(jax.random.fold_in(streams_of[6], 71), 0)
    return {"panel": panel, "eigenvalues": eigenvalues, "positions": positions, "elements": elements, "radii": radii, "neighbors": neighbors}


def atom_radius(elements, radii):
    table = (elements[None, :] == jnp.arange(radii.shape[0], dtype=jnp.int32)[:, None]).astype(jnp.float32)
    return lax.optimization_barrier(jnp.sum(table * radii[:, None], axis=0))

def tile_forces(scaled_own, panel_ext, geo_own, geo_ext, nbr_rows, base_tile, tile_size):
    modes = panel_ext.shape[0]
    ext_tiles = panel_ext.reshape(modes, -1, 3 * tile_size)
    geo_tiles = geo_ext.reshape(4, -1, tile_size)
    own_tiles = scaled_own.reshape(modes, -1, 3 * tile_size)
    own_geo = geo_own.reshape(4, -1, tile_size)

    def one_tile(index):
        left = own_tiles[:, index, :].astype(jnp.float32)
        local = nbr_rows[index] - base_tile
        slabs = jnp.take(ext_tiles, local, axis=1).astype(jnp.float32)
        coupling = jnp.einsum('pm,pkn->kmn', left, slabs, precision=lax.Precision.HIGHEST)
        count = local.shape[0]
        coupling = coupling.reshape(count, 3, tile_size, 3, tile_size)
        geo_i = own_geo[:, index, :]
        geo_j = jnp.take(geo_tiles, local, axis=1)
        delta = geo_i[:3, None, :, None] - geo_j[:3, :, None, :]
        spread = geo_i[3][None, :, None] + geo_j[3][:, None, :]
        inverse = 1.0 / (lax.optimization_barrier(jnp.sum(delta * delta, axis=0)) + spread * spread)
        fifth = inverse * inverse * jnp.sqrt(inverse)
        seventh = fifth * inverse
        trace = jnp.einsum('kaiaj->kij', coupling)
        along = jnp.einsum('kcibj,bkij->ckij', coupling, delta)
        across = jnp.einsum('kaicj,akij->ckij', coupling, delta)
        quad = jnp.einsum('akij,kaibj,bkij->kij', delta, coupling, delta)
        term = 3.0 * fifth * (trace * delta + along + across) - 15.0 * seventh * quad * delta
        return -lax.optimization_barrier(jnp.sum(term, axis=(1, 3)))
    count_tiles = own_tiles.shape[1]
    result = lax.map(one_tile, jnp.arange(count_tiles, dtype=jnp.int32))
    return jnp.transpose(result, (1, 0, 2)).reshape(3, -1)

def reference(panel, eigenvalues, positions, elements, radii, neighbors):
    weights = 0.25 / jnp.sqrt(eigenvalues)
    scaled = (panel.astype(jnp.float32) * weights[:, None]).astype(jnp.bfloat16)
    geometry = jnp.concatenate([positions, atom_radius(elements, radii)[None, :]], axis=0)
    return tile_forces(scaled, panel, geometry, geometry, neighbors, 0, BLK)
```

```python
import jax
import jax.numpy as jnp
from jax import lax
from jax.experimental import pallas as pl
from jax.experimental.pallas import tpu as pltpu
from jax.sharding import PartitionSpec as P

BLK = 128
OWN = 24
HALF = 12
LOCAL = OWN + 2 * HALF
SLOTS = 5
DEPTH = 96
WIDTH = 3 * BLK
UNROLL = 4
F32 = jnp.float32
BF16 = jnp.bfloat16


def products(i, j, left, right, out):
    zero = jnp.zeros((DEPTH, BLK), BF16)
    for slot, (a, b, first) in enumerate(((0, 1, True), (0, 2, False), (1, 2, True))):
        col_a, col_b = right[i, a], right[i, b]
        if first:
            diag = jnp.concatenate([col_a * BF16(2), zero], axis=0)
        else:
            diag = jnp.concatenate([zero, col_b * BF16(2)], axis=0)
        rhs = jnp.concatenate([jnp.concatenate([col_b, col_a], axis=0), diag], axis=1)
        res = lax.dot_general(
            left[j, slot], rhs, (((1,), (0,)), ((), ())), preferred_element_type=F32
        )
        out[2 * slot] = res[:, :BLK]
        out[2 * slot + 1] = res[:, BLK:]


def contract(dest, i, j, mats, geo_row, geo_col, acc):
    own = [jnp.broadcast_to(geo_row[i, c : c + 1, :], (8, BLK)) for c in range(4)]
    total = [None, None, None]
    for strip in range(BLK // 8):
        at = pl.ds(8 * strip, 8)
        cols = geo_col[j, at, :]
        other = [jnp.broadcast_to(cols[:, c : c + 1], (8, BLK)) for c in range(4)]
        d = [own[c] - other[c] for c in range(3)]
        s = own[3] + other[3]
        m01, m00, m02, m22, m12, m11 = (mats[k, at, :] for k in range(6))
        u = (d[0] * d[0] + d[1] * d[1]) + (d[2] * d[2] + s * s)
        y = lax.rsqrt(u)
        y2 = y * y
        f5 = y2 * y2 * y
        v0 = m00 * d[0] + m01 * d[1] + m02 * d[2]
        v1 = m01 * d[0] + m11 * d[1] + m12 * d[2]
        v2 = m02 * d[0] + m12 * d[1] + m22 * d[2]
        q = d[0] * v0 + d[1] * v1 + d[2] * v2
        w = (m00 + m11 + m22) * 0.5 - (y2 * 2.5) * q
        for c, v in enumerate((v0, v1, v2)):
            term = f5 * (v + d[c] * w)
            total[c] = term if total[c] is None else total[c] + term
    for c in range(3):
        acc[dest, c] = acc[dest, c] + total[c]


def prepare(tile, src, geo, first, gain, left, right, geo_row, geo_col):
    parts = [
        src[:, pl.ds(pl.multiple_of(first * WIDTH + c * BLK, BLK), BLK)] for c in range(3)
    ]
    for c in range(3):
        right[tile, c] = (parts[c].astype(F32) * gain[...]).astype(BF16)
    for slot, (a, b) in enumerate(((0, 1), (0, 2), (1, 2))):
        left[tile, slot] = jnp.concatenate([parts[a], parts[b]], axis=0).T
    prepare_geo(tile, geo, first, geo_row, geo_col)


def prepare_geo(tile, geo, first, geo_row, geo_col):
    rows = geo[:, pl.ds(pl.multiple_of(first * BLK, BLK), BLK)]
    geo_row[tile] = rows
    geo_col[tile] = jnp.concatenate([rows, jnp.zeros((BLK - 8, BLK), F32)], axis=0).T


def run_pairs(count, pairs, left, right, geo_row, geo_col, mats, acc):
    def fields(code):
        return code // 4096, (code // 64) % 64, code % 64

    trash = LOCAL * 4096 + HALF * 64 + HALF
    for k in range(UNROLL):
        pairs[count + k] = trash
    _, i, j = fields(pairs[0])
    products(i, j, left, right, mats[0])

    @pl.loop(0, (count + UNROLL - 1) // UNROLL)
    def _(step):
        todo = [fields(pairs[step * UNROLL + k]) for k in range(UNROLL + 1)]
        for k in range(UNROLL):
            products(todo[k + 1][1], todo[k + 1][2], left, right, mats[(k + 1) % 2])
            contract(*todo[k], mats[k % 2], geo_row, geo_col, acc)


def append(pairs, count, keep, i, j):
    pairs[count] = i * 4096 + i * 64 + jnp.clip(j, 0, LOCAL - 1)
    return count + keep.astype(jnp.int32)


def own_kernel(
    row, nbr, panel, geo, gain, acc, left, right, pairs, geo_row, geo_col, mat_a, mat_b
):
    acc[...] = jnp.zeros_like(acc)
    shift = HALF - row[0] * OWN

    def scan(index, count):
        i = HALF + index // SLOTS
        j = nbr[index] + shift
        return append(pairs, count, (j >= HALF) & (j < HALF + OWN), i, j)

    count = lax.fori_loop(0, OWN * SLOTS, scan, jnp.int32(0))

    @pl.loop(0, OWN // 2)
    def _(step):
        for k in range(2):
            t = 2 * step + k
            prepare(
                t, panel, geo, t, gain, left, right,
                geo_row.at[pl.ds(HALF, OWN)], geo_col.at[pl.ds(HALF, OWN)],
            )

    class Shifted:
        def __init__(self, ref):
            self.ref = ref

        def __getitem__(self, at):
            return self.ref[(at[0] - HALF,) + at[1:]]

    run_pairs(
        count, pairs, Shifted(left), Shifted(right), geo_row, geo_col, (mat_a, mat_b), acc
    )


def rest_kernel(
    row, nbr, nbr_lo, nbr_hi, start, left_own, right_own, lo, hi, geo, geo_lo, geo_hi, gain,
    out, pairs, acc, left, right, geo_row, geo_col, mat_a, mat_b, sems,
):
    own = pl.ds(HALF, OWN)
    copies = [
        pltpu.make_async_copy(left_own, left.at[own], sems.at[0]),
        pltpu.make_async_copy(right_own, right.at[own], sems.at[1]),
    ]
    for copy in copies:
        copy.start()
    acc[...] = start[...]
    r = row[0]
    shift = HALF - r * OWN

    def scan_own(index, count):
        i = HALF + index // SLOTS
        j = nbr[index] + shift
        low = (j >= 0) & (j < HALF) & (i >= 2 * HALF)
        high = (j >= HALF + OWN) & (j < LOCAL)
        return append(pairs, count, low | high, i, j)

    def scan_lo(index, count):
        j = nbr_lo[index] + shift
        keep = (j >= 2 * HALF) & (j < HALF + OWN) & (r > 0)
        return append(pairs, count, keep, index // SLOTS, j)

    def scan_hi(index, count):
        j = nbr_hi[index] + shift
        keep = (j >= HALF) & (j < HALF + OWN) & (r < 15)
        return append(pairs, count, keep, HALF + OWN + index // SLOTS, j)

    count = lax.fori_loop(0, OWN * SLOTS, scan_own, jnp.int32(0))
    count = lax.fori_loop(0, HALF * SLOTS, scan_lo, count)
    count = lax.fori_loop(0, HALF * SLOTS, scan_hi, count)

    @pl.loop(0, HALF)
    def _(t):
        prepare(t, lo, geo_lo, t, gain, left, right, geo_row, geo_col)
        prepare(HALF + OWN + t, hi, geo_hi, t, gain, left, right, geo_row, geo_col)
        for k in range(2):
            prepare_geo(HALF + 2 * t + k, geo, 2 * t + k, geo_row, geo_col)

    for copy in copies:
        copy.wait()
    run_pairs(count, pairs, left, right, geo_row, geo_col, (mat_a, mat_b), acc)
    for t in range(LOCAL):
        out[t] = -3.0 * jnp.sum(acc[t], axis=1)


VMEM = pl.BlockSpec(memory_space=pltpu.VMEM)
SMEM = pl.BlockSpec(memory_space=pltpu.SMEM)
ANY = pl.BlockSpec(memory_space=pl.ANY)
PARAMS = pltpu.CompilerParams(vmem_limit_bytes=48 << 20)


def stacks(tiles):
    return (tiles, 3, BLK, 2 * DEPTH), (tiles, 3, DEPTH, BLK)


def cost(pairs):
    return pl.CostEstimate(
        flops=pairs * 2 * 3 * BLK * 2 * BLK * 2 * DEPTH, bytes_accessed=8 << 20, transcendentals=0
    )


def own_call(row, nbr, panel, geo, gain):
    left, right = stacks(OWN)
    return pl.pallas_call(
        own_kernel,
        out_shape=(
            jax.ShapeDtypeStruct((LOCAL + 1, 3, 8, BLK), F32),
            jax.ShapeDtypeStruct(left, BF16),
            jax.ShapeDtypeStruct(right, BF16),
        ),
        in_specs=[SMEM, SMEM, VMEM, VMEM, VMEM],
        out_specs=(VMEM, VMEM, VMEM),
        scratch_shapes=[
            pltpu.SMEM((OWN * SLOTS + UNROLL + 4,), jnp.int32),
            pltpu.VMEM((LOCAL, 8, BLK), F32),
            pltpu.VMEM((LOCAL, BLK, BLK), F32),
            pltpu.VMEM((6, BLK, BLK), F32),
            pltpu.VMEM((6, BLK, BLK), F32),
        ],
        compiler_params=PARAMS,
        cost_estimate=cost(40),
        name="own_pairs",
    )(row, nbr, panel, geo, gain)


def rest_call(row, nbr, nbr_lo, nbr_hi, start, left_own, right_own, lo, hi, geo, geo_lo, geo_hi, gain):
    left, right = stacks(LOCAL)
    return pl.pallas_call(
        rest_kernel,
        out_shape=jax.ShapeDtypeStruct((LOCAL, 3, BLK), F32),
        in_specs=[SMEM] * 4 + [VMEM, ANY, ANY] + [VMEM] * 6,
        out_specs=VMEM,
        scratch_shapes=[
            pltpu.SMEM((2 * OWN * SLOTS + UNROLL + 4,), jnp.int32),
            pltpu.VMEM((LOCAL + 1, 3, 8, BLK), F32),
            pltpu.VMEM(left, BF16),
            pltpu.VMEM(right, BF16),
            pltpu.VMEM((LOCAL, 8, BLK), F32),
            pltpu.VMEM((LOCAL, BLK, BLK), F32),
            pltpu.VMEM((6, BLK, BLK), F32),
            pltpu.VMEM((6, BLK, BLK), F32),
            pltpu.SemaphoreType.DMA((2,)),
        ],
        compiler_params=PARAMS,
        cost_estimate=cost(80),
        name="rest_pairs",
    )(row, nbr, nbr_lo, nbr_hi, start, left_own, right_own, lo, hi, geo, geo_lo, geo_hi, gain)


def atom_radius(elements, radii):
    table = (elements[None, :] == jnp.arange(radii.shape[0], dtype=jnp.int32)[:, None]).astype(F32)
    return jnp.sum(table * radii[:, None], axis=0)


def per_device(panel, eigenvalues, positions, elements, radii, neighbors):
    rows = lax.axis_size("row")
    up = [(k, k + 1) for k in range(rows - 1)]
    down = [(k + 1, k) for k in range(rows - 1)]
    atoms = HALF * BLK
    nbr = neighbors.reshape(-1)
    near = HALF * SLOTS

    radius = atom_radius(elements, radii)
    listed = jnp.pad(nbr.astype(F32).reshape(2, near), ((0, 0), (0, atoms - near))).reshape(1, -1)
    geo = jnp.concatenate([positions, radius[None, :], listed, jnp.zeros((3, 2 * atoms), F32)], axis=0)
    geo_lo = lax.ppermute(geo[:, atoms:], "row", up)
    geo_hi = lax.ppermute(geo[:, :atoms], "row", down)
    lo = lax.ppermute(panel[:, HALF * WIDTH :], "row", up)
    hi = lax.ppermute(panel[:, : HALF * WIDTH], "row", down)

    gain = jnp.broadcast_to((0.25 / jnp.sqrt(eigenvalues))[:, None], (DEPTH, BLK))
    row = lax.axis_index("row").astype(jnp.int32).reshape(1)
    start, left_own, right_own = own_call(row, nbr, panel, geo, gain)
    nbr_lo = geo_lo[4, :near].astype(jnp.int32)
    nbr_hi = geo_hi[4, :near].astype(jnp.int32)
    forces = rest_call(
        row, nbr, nbr_lo, nbr_hi, start, left_own, right_own, lo, hi, geo, geo_lo, geo_hi, gain
    )

    from_below = lax.ppermute(forces[HALF + OWN :], "row", up)
    from_above = lax.ppermute(forces[:HALF], "row", down)
    part = forces[HALF : HALF + OWN] + jnp.concatenate([from_below, from_above], axis=0)

    me = lax.axis_index("col")
    cols = lax.axis_size("col")
    for bit in (8, 4, 2, 1):
        if bit == 1:
            part = jnp.transpose(part, (1, 0, 2)).reshape(3, 3 * BLK)
            halves = part[:, : 3 * BLK // 2], part[:, 3 * BLK // 2 :]
        else:
            count = part.shape[0] // 2
            halves = part[:count], part[count:]
        high = (me // bit) % 2 == 1
        sent = jnp.where(high, halves[0], halves[1])
        kept = jnp.where(high, halves[1], halves[0])
        part = kept + lax.ppermute(sent, "col", [(k, k ^ bit) for k in range(cols)])
    return part


def solution(mesh):
    return jax.shard_map(
        per_device,
        mesh=mesh,
        in_specs=(P("col", "row"), P("col"), P(None, "row"), P("row"), P(), P("row", None)),
        out_specs=P(None, ("row", "col")),
        check_vma=False,
    )
```

```python
import functools

import jax
import jax.numpy as jnp
from jax import lax
from jax.experimental import pallas as pl
from jax.experimental.pallas import tpu as pltpu
from jax.sharding import PartitionSpec as P

BLK = 128
OWN = 24
HALF = 12
TRASH = 2 * OWN
LOCAL = OWN + 2 * HALF
SLOTS = 5
DEPTH = 96
WIDTH = 3 * BLK
UNROLL = 4
F32 = jnp.float32
BF16 = jnp.bfloat16


def products(i, j, left, right, out):
    zero = jnp.zeros((DEPTH, BLK), BF16)
    for slot, (a, b, first) in enumerate(((0, 1, True), (0, 2, False), (1, 2, True))):
        col_a, col_b = right[i, a], right[i, b]
        if first:
            diag = jnp.concatenate([col_a * BF16(2), zero], axis=0)
        else:
            diag = jnp.concatenate([zero, col_b * BF16(2)], axis=0)
        rhs = jnp.concatenate([jnp.concatenate([col_b, col_a], axis=0), diag], axis=1)
        res = lax.dot_general(
            left[j, slot], rhs, (((1,), (0,)), ((), ())), preferred_element_type=F32
        )
        out[2 * slot] = res[:, :BLK]
        out[2 * slot + 1] = res[:, BLK:]


def contract(dest, i, j, mats, geo_row, geo_col, acc, back=None, turned=None):
    own = [jnp.broadcast_to(geo_row[i, c : c + 1, :], (8, BLK)) for c in range(4)]
    total = [None, None, None]
    for strip in range(BLK // 8):
        at = pl.ds(8 * strip, 8)
        cols = geo_col[j, at, :]
        other = [jnp.broadcast_to(cols[:, c : c + 1], (8, BLK)) for c in range(4)]
        d = [own[c] - other[c] for c in range(3)]
        s = own[3] + other[3]
        m01, m00, m02, m22, m12, m11 = (mats[k, at, :] for k in range(6))
        u = (d[0] * d[0] + d[1] * d[1]) + (d[2] * d[2] + s * s)
        y = lax.rsqrt(u)
        y2 = y * y
        f5 = y2 * y2 * y
        v0 = m00 * d[0] + m01 * d[1] + m02 * d[2]
        v1 = m01 * d[0] + m11 * d[1] + m12 * d[2]
        v2 = m02 * d[0] + m12 * d[1] + m22 * d[2]
        q = d[0] * v0 + d[1] * v1 + d[2] * v2
        w = (m00 + m11 + m22) * 0.5 - (y2 * 2.5) * q
        terms = [f5 * (v + d[c] * w) for c, v in enumerate((v0, v1, v2))]
        for c, term in enumerate(terms):
            total[c] = term if total[c] is None else total[c] + term
        if turned is not None:
            for c, term in enumerate(terms):
                turned[c, at, :] = term
    for c in range(3):
        acc[dest, c] = acc[dest, c] + total[c]
    if turned is not None:
        for c in range(3):
            flipped = jnp.sum(turned[c].T.reshape(BLK // 8, 8, BLK), axis=0)
            acc[back, c] = acc[back, c] - flipped


def split(src, first):
    at = pl.multiple_of(first * WIDTH, BLK)
    return [src[:, pl.ds(at + c * BLK, BLK)] for c in range(3)]


def turn_parts(tile, parts, left):
    for slot, (a, b) in enumerate(((0, 1), (0, 2), (1, 2))):
        left[tile, slot] = jnp.concatenate([parts[a], parts[b]], axis=0).T


def turned_geo(rows):
    return jnp.concatenate([rows, jnp.zeros((BLK - 8, BLK), F32)], axis=0).T


def encode(dest, back, i, j):
    return dest * 32768 + back * 512 + i * 16 + j


def decode(code):
    return code >> 15, (code >> 9) & 63, (code >> 4) & 31, code & 15


def steps(count, todo_of, left, right, geo_row, geo_col, mats, acc, turned=None, before=None):
    _, _, i, j = todo_of(jnp.int32(0))
    products(i, j, left, right, mats[0])

    def body(step, carry):
        if before is not None:
            carry = before(step, carry)
        todo = [todo_of(step * UNROLL + k) for k in range(UNROLL + 1)]
        for k in range(UNROLL):
            products(todo[k + 1][2], todo[k + 1][3], left, right, mats[(k + 1) % 2])
            dest, back, i, j = todo[k]
            turn = None if turned is None else turned[k % 2]
            contract(dest, i, j, mats[k % 2], geo_row, geo_col, acc, back, turn)
        return carry

    return lax.fori_loop(0, (count + UNROLL - 1) // UNROLL, body, jnp.int32(0))


def pack_kernel(
    panel_hbm, positions_hbm, elements_hbm, radii_hbm, nbr_hbm, geo, lower, upper,
    panel, ext, positions, elements, radii, nbr, sems,
):
    width = HALF * WIDTH
    small = [
        pltpu.make_async_copy(src, dst, sems.at[k])
        for k, (src, dst) in enumerate(
            ((positions_hbm, positions), (elements_hbm, elements), (radii_hbm, radii), (nbr_hbm, nbr))
        )
    ]
    halves = [
        pltpu.make_async_copy(
            panel_hbm.at[:, pl.ds(width * k, width)], panel.at[:, pl.ds(width * k, width)], sems.at[4 + k]
        )
        for k in range(2)
    ]
    for copy in small + [halves[1], halves[0]]:
        copy.start()
    for copy in small:
        copy.wait()
    kinds = elements[...]
    radius = jnp.zeros((OWN, BLK), F32)
    for kind in range(radii.shape[1]):
        radius = jnp.where(kinds == kind, radii[0:1, kind : kind + 1], radius)
    listed = nbr[...].astype(F32)
    listed = jnp.concatenate([listed, jnp.zeros((SLOTS, BLK - OWN), F32)], axis=1)
    listed = jnp.concatenate([listed, jnp.zeros((BLK - SLOTS, BLK), F32)], axis=0).T
    copies = []
    for k, out in ((1, upper), (0, lower)):
        tiles = []
        for t in range(HALF * k, HALF * k + HALF):
            rows = jnp.concatenate(
                [
                    positions[:, t * BLK : (t + 1) * BLK],
                    radius[t : t + 1],
                    listed[t : t + 1],
                    jnp.zeros((3, BLK), F32),
                ],
                axis=0,
            )
            geo[t] = rows
            tiles.append(rows)
        rest = jnp.concatenate(tiles, axis=0)
        for part in range(3):
            coarse = rest.astype(BF16)
            rest = rest - coarse.astype(F32)
            ext[k, :, part * BLK : (part + 1) * BLK] = coarse
        copies.append(
            pltpu.make_async_copy(ext.at[k], out.at[:, pl.ds(width, WIDTH)], sems.at[6 + k])
        )
        copies[-1].start()
    for k, out in ((1, upper), (0, lower)):
        halves[k].wait()
        copies.append(
            pltpu.make_async_copy(
                panel.at[:, pl.ds(width * k, width)], out.at[:, pl.ds(0, width)], sems.at[8 + k]
            )
        )
        copies[-1].start()
    for copy in copies:
        copy.wait()


def own_kernel(
    row, panel, geo, gain, out, right, left, geo_col, pairs, near, near_all, acc, mat_a, mat_b, sem
):
    near_all[...] = geo[:, 4, :].astype(jnp.int32)
    fetch = pltpu.make_async_copy(near_all, near, sem.at[0])
    fetch.start()
    acc[...] = jnp.zeros_like(acc)
    fetch.wait()
    first = row[0] * OWN

    def step(index, count):
        for k in range(3):
            t = 3 * index + k
            parts = split(panel, t)
            turn_parts(t, parts, left)
            for c in range(3):
                right[t, c] = (parts[c].astype(F32) * gain[...]).astype(BF16)
            geo_col[t] = turned_geo(geo[t])
            for slot in range(SLOTS):
                j = near[t, slot] - first
                pairs[count] = encode(t, 0, t, 0) + j
                count = count + ((j >= 0) & (j < OWN)).astype(jnp.int32)
        return count

    def todo_of(n):
        code = pairs[n]
        dest = code >> 15
        return dest, 0, jnp.minimum(dest, OWN - 1), (code & 511) - 16 * jnp.minimum(dest, OWN - 1)

    count = lax.fori_loop(0, OWN // 3, step, jnp.int32(0))
    for k in range(UNROLL):
        pairs[count + k] = encode(OWN, 0, OWN - 1, 0)
    steps(count, todo_of, left, right, geo, geo_col, (mat_a, mat_b), acc)
    out[...] = acc[pl.ds(0, OWN)]


def side_kernel(high, row, start, right, message, geo, out, *scratch):
    pairs, near, near_all, acc, left, geo_col, turn_a, turn_b, mat_a, mat_b, sem = scratch
    width = HALF * WIDTH
    rows = [message[:, width + k * BLK : width + (k + 1) * BLK].astype(F32) for k in range(3)]
    halo = (rows[0] + rows[1] + rows[2]).reshape(HALF, 8, BLK)
    near_all[pl.ds(0, OWN)] = geo[:, 4, :].astype(jnp.int32)
    near_all[pl.ds(OWN, 16)] = jnp.concatenate(
        [halo[:, 4, :].astype(jnp.int32), jnp.zeros((4, BLK), jnp.int32)], axis=0
    )
    fetch = pltpu.make_async_copy(near_all, near, sem.at[0])
    fetch.start()
    for t in range(HALF):
        geo_col[t] = turned_geo(halo[t])
    if high:
        acc[...] = start[...]
    else:
        acc[pl.ds(0, OWN)] = start[...]
        acc[pl.ds(OWN, OWN + 1)] = jnp.zeros((OWN + 1, 3, 8, BLK), F32)

    @pl.loop(0, HALF // 4)
    def _(step):
        for k in range(4):
            turn_parts(4 * step + k, split(message, 4 * step + k), left)

    r = row[0]
    first = r * OWN
    base = 0 if high else HALF
    exists = (r < 15) if high else (r > 0)

    def facing(n):
        n = jnp.minimum(n, HALF - 1)
        return base + n, OWN + base + n, base + n, n

    def scan(step, count):
        for slot in range(2, SLOTS):
            for k in range(4):
                h = 4 * step + k
                i = near[OWN + h, slot] - first
                pairs[count] = encode(TRASH, OWN + base + h, i, h)
                keep = exists & (i >= base) & (i < OWN)
                count = count + keep.astype(jnp.int32)
                for t in (h, HALF + h) if high else (HALF + h,):
                    j = near[t, slot] - first - (OWN if high else -HALF)
                    pairs[count] = encode(t, TRASH, t, j)
                    count = count + ((j >= 0) & (j < HALF)).astype(jnp.int32)
        return count

    fetch.wait()
    rest = (left, right, geo, geo_col, (mat_a, mat_b), acc, (turn_a, turn_b))
    count = steps(HALF, facing, *rest, before=scan)
    for k in range(UNROLL):
        pairs[count + k] = encode(TRASH, TRASH, 0, 0)
    steps(count, lambda n: decode(pairs[n]), *rest)
    if not high:
        out[...] = acc[...]
        return
    for m in range(OWN // 3):
        for part in range(2):
            tiles = []
            for t in range(3 * m, 3 * m + 3):
                tiles.append(-3.0 * jnp.sum(acc[OWN * part + t], axis=1))
            line = jnp.concatenate(tiles, axis=1)
            half = 3 * BLK // 2
            out[2 * m, pl.ds(3 * part, 3)] = line[:, :half]
            out[2 * m + 1, pl.ds(3 * part, 3)] = line[:, half:]


VMEM = pl.BlockSpec(memory_space=pltpu.VMEM)
SMEM = pl.BlockSpec(memory_space=pltpu.SMEM)
ANY = pl.BlockSpec(memory_space=pl.ANY)


def stacks(tiles):
    return (tiles, 3, BLK, 2 * DEPTH), (tiles, 3, DEPTH, BLK)


def cost(pairs):
    return pl.CostEstimate(
        flops=pairs * 2 * 3 * BLK * 2 * BLK * 2 * DEPTH, bytes_accessed=8 << 20, transcendentals=0
    )


def own_call(row, panel, geo, gain):
    left, right = stacks(OWN)
    return pl.pallas_call(
        own_kernel,
        out_shape=(
            jax.ShapeDtypeStruct((OWN, 3, 8, BLK), F32),
            jax.ShapeDtypeStruct(right, BF16),
        ),
        in_specs=[SMEM, VMEM, VMEM, VMEM],
        out_specs=(VMEM, VMEM),
        scratch_shapes=[
            pltpu.VMEM(left, BF16),
            pltpu.VMEM((OWN, BLK, BLK), F32),
            pltpu.SMEM((OWN * SLOTS + UNROLL + 4,), jnp.int32),
            pltpu.SMEM((OWN, BLK), jnp.int32),
            pltpu.VMEM((OWN, BLK), jnp.int32),
            pltpu.VMEM((OWN + 1, 3, 8, BLK), F32),
            pltpu.VMEM((6, BLK, BLK), F32),
            pltpu.VMEM((6, BLK, BLK), F32),
            pltpu.SemaphoreType.DMA((1,)),
        ],
        compiler_params=pltpu.CompilerParams(vmem_limit_bytes=20 << 20),
        cost_estimate=cost(40),
        name="own_pairs",
    )(row, panel, geo, gain)


def side_call(high, *args):
    left, _ = stacks(HALF)
    if high:
        shape = jax.ShapeDtypeStruct((2 * OWN // 3, 6, 3 * BLK // 2), F32)
    else:
        shape = jax.ShapeDtypeStruct((TRASH + 1, 3, 8, BLK), F32)
    return pl.pallas_call(
        functools.partial(side_kernel, high),
        out_shape=shape,
        in_specs=[SMEM] + [VMEM] * 4,
        out_specs=VMEM,
        scratch_shapes=[
            pltpu.SMEM((3 * HALF * (SLOTS - 2) + UNROLL + 4,), jnp.int32),
            pltpu.SMEM((OWN + 16, BLK), jnp.int32),
            pltpu.VMEM((OWN + 16, BLK), jnp.int32),
            pltpu.VMEM((TRASH + 1, 3, 8, BLK), F32),
            pltpu.VMEM(left, BF16),
            pltpu.VMEM((HALF, BLK, BLK), F32),
            pltpu.VMEM((3, BLK, BLK), F32),
            pltpu.VMEM((3, BLK, BLK), F32),
            pltpu.VMEM((6, BLK, BLK), F32),
            pltpu.VMEM((6, BLK, BLK), F32),
            pltpu.SemaphoreType.DMA((1,)),
        ],
        compiler_params=pltpu.CompilerParams(vmem_limit_bytes=20 << 20),
        cost_estimate=cost(30),
        name="above_pairs" if high else "below_pairs",
    )(*args)


def pack_call(panel, positions, elements, radii, nbr):
    message = jax.ShapeDtypeStruct((DEPTH, (HALF + 1) * WIDTH), BF16)
    return pl.pallas_call(
        pack_kernel,
        out_shape=(jax.ShapeDtypeStruct((OWN, 8, BLK), F32), message, message),
        in_specs=[ANY] * 5,
        out_specs=(VMEM, ANY, ANY),
        scratch_shapes=[
            pltpu.VMEM(panel.shape, BF16),
            pltpu.VMEM((2, DEPTH, WIDTH), BF16),
            pltpu.VMEM(positions.shape, F32),
            pltpu.VMEM(elements.shape, jnp.int32),
            pltpu.VMEM(radii.shape, F32),
            pltpu.VMEM(nbr.shape, jnp.int32),
            pltpu.SemaphoreType.DMA((10,)),
        ],
        compiler_params=pltpu.CompilerParams(vmem_limit_bytes=56 << 20),
        name="pack",
    )(panel, positions, elements, radii, nbr)


def per_device(panel, eigenvalues, positions, elements, radii, neighbors):
    rows = lax.axis_size("row")
    up = [(k, k + 1) for k in range(rows - 1)]
    down = [(k + 1, k) for k in range(rows - 1)]
    geo, lower, upper = pack_call(
        panel, positions, elements.reshape(OWN, BLK), radii[None], neighbors.T
    )
    lo = lax.ppermute(upper, "row", up)
    hi = lax.ppermute(lower, "row", down)

    gain = jnp.broadcast_to((0.25 / jnp.sqrt(eigenvalues))[:, None], (DEPTH, BLK))
    row = lax.axis_index("row").astype(jnp.int32).reshape(1)
    start, right = own_call(row, panel, geo, gain)
    start = side_call(False, row, start, right, lo, geo)
    forces = side_call(True, row, start, right, hi, geo)

    cols = lax.axis_size("col")
    part = jnp.sum(lax.all_to_all(forces, "col", 0, 0, tiled=True), axis=0)
    back = []
    for k in range(rows):
        for c in range(cols):
            to = k + 1 if c < cols // 2 else k - 1
            if 0 <= to < rows:
                back.append((k * cols + c, to * cols + c))
    return part[:3] + lax.ppermute(part[3:], ("row", "col"), back)


def solution(mesh):
    return jax.shard_map(
        per_device,
        mesh=mesh,
        in_specs=(P("col", "row"), P("col"), P(None, "row"), P("row"), P(), P("row", None)),
        out_specs=P(None, ("row", "col")),
        check_vma=False,
    )
```

```python
import functools

import jax
import jax.numpy as jnp
from jax import lax
from jax.experimental import pallas as pl
from jax.experimental.pallas import tpu as pltpu
from jax.sharding import PartitionSpec as P

BLK = 128
OWN = 24
HALF = 12
TRASH = 2 * OWN
LOCAL = OWN + 2 * HALF
SLOTS = 5
DEPTH = 96
WIDTH = 3 * BLK
UNROLL = 4
F32 = jnp.float32
BF16 = jnp.bfloat16


def products(i, j, left, right, out):
    zero = jnp.zeros((DEPTH, BLK), BF16)
    for slot, (a, b, first) in enumerate(((0, 1, True), (0, 2, False), (1, 2, True))):
        col_a, col_b = right[i, a], right[i, b]
        if first:
            diag = jnp.concatenate([col_a * BF16(2), zero], axis=0)
        else:
            diag = jnp.concatenate([zero, col_b * BF16(2)], axis=0)
        rhs = jnp.concatenate([jnp.concatenate([col_b, col_a], axis=0), diag], axis=1)
        res = lax.dot_general(
            left[j, slot], rhs, (((1,), (0,)), ((), ())), preferred_element_type=F32
        )
        out[2 * slot] = res[:, :BLK]
        out[2 * slot + 1] = res[:, BLK:]


def contract(dest, i, j, mats, geo_row, geo_col, acc, back=None, turned=None):
    own = [jnp.broadcast_to(geo_row[i, c : c + 1, :], (8, BLK)) for c in range(4)]
    total = [None, None, None]
    for strip in range(BLK // 8):
        at = pl.ds(8 * strip, 8)
        other = [geo_col[j, c, at, :] for c in range(4)]
        d = [own[c] - other[c] for c in range(3)]
        s = own[3] + other[3]
        m01, m00, m02, m22, m12, m11 = (mats[k, at, :] for k in range(6))
        u = (d[0] * d[0] + d[1] * d[1]) + (d[2] * d[2] + s * s)
        y = lax.rsqrt(u)
        y2 = y * y
        f5 = y2 * y2 * y
        v0 = m00 * d[0] + m01 * d[1] + m02 * d[2]
        v1 = m01 * d[0] + m11 * d[1] + m12 * d[2]
        v2 = m02 * d[0] + m12 * d[1] + m22 * d[2]
        q = d[0] * v0 + d[1] * v1 + d[2] * v2
        w = (m00 + m11 + m22) * 0.5 - (y2 * 2.5) * q
        terms = [f5 * (v + d[c] * w) for c, v in enumerate((v0, v1, v2))]
        for c, term in enumerate(terms):
            total[c] = term if total[c] is None else total[c] + term
        if turned is not None:
            for c, term in enumerate(terms):
                turned[c, at, :] = term
    for c in range(3):
        acc[dest, c] = acc[dest, c] + total[c]
    if turned is not None:
        for c in range(3):
            flipped = jnp.sum(turned[c].T.reshape(BLK // 8, 8, BLK), axis=0)
            acc[back, c] = acc[back, c] - flipped


def split(src, first):
    at = pl.multiple_of(first * WIDTH, BLK)
    return [src[:, pl.ds(at + c * BLK, BLK)] for c in range(3)]


def turn_parts(tile, parts, left):
    for slot, (a, b) in enumerate(((0, 1), (0, 2), (1, 2))):
        left[tile, slot] = jnp.concatenate([parts[a], parts[b]], axis=0).T


def turned_geo(rows):
    return jnp.concatenate([rows, jnp.zeros((BLK - 8, BLK), F32)], axis=0).T


def encode(dest, back, own, halo):
    return dest * 32768 + back * 512 + own * 16 + halo


def decode(code):
    return code >> 15, (code >> 9) & 63, code & 15, (code >> 4) & 31


class Columns:
    def __init__(self, ref):
        self.ref = ref

    def __getitem__(self, at):
        tile, c = at
        return self.ref[:, pl.ds(pl.multiple_of(tile * WIDTH + c * BLK, BLK), BLK)]


def steps(count, todo_of, left, right, geo_row, geo_col, mats, acc, turned=None, before=None):
    _, _, i, j = todo_of(jnp.int32(0))
    products(i, j, left, right, mats[0])

    def body(step, carry):
        if before is not None:
            carry = before(step, carry)
        todo = [todo_of(step * UNROLL + k) for k in range(UNROLL + 1)]
        for k in range(UNROLL):
            products(todo[k + 1][2], todo[k + 1][3], left, right, mats[(k + 1) % 2])
            dest, back, i, j = todo[k]
            turn = None if turned is None else turned[k % 2]
            contract(dest, i, j, mats[k % 2], geo_row, geo_col, acc, back, turn)
        return carry

    return lax.fori_loop(0, (count + UNROLL - 1) // UNROLL, body, jnp.int32(0))


def pack_kernel(
    panel_hbm, positions_hbm, elements_hbm, radii_hbm, nbr_hbm, geo, lower, upper,
    panel, ext, positions, elements, radii, nbr, sems,
):
    width = HALF * WIDTH
    small = [
        pltpu.make_async_copy(src, dst, sems.at[k])
        for k, (src, dst) in enumerate(
            ((positions_hbm, positions), (elements_hbm, elements), (radii_hbm, radii), (nbr_hbm, nbr))
        )
    ]
    halves = [
        pltpu.make_async_copy(
            panel_hbm.at[:, pl.ds(width * k, width)], panel.at[:, pl.ds(width * k, width)], sems.at[4 + k]
        )
        for k in range(2)
    ]
    for copy in small + [halves[1], halves[0]]:
        copy.start()
    for copy in small:
        copy.wait()
    kinds = elements[...]
    radius = jnp.zeros((OWN, BLK), F32)
    for kind in range(radii.shape[1]):
        radius = jnp.where(kinds == kind, radii[0:1, kind : kind + 1], radius)
    listed = nbr[...].astype(F32)
    listed = jnp.concatenate([listed, jnp.zeros((SLOTS, BLK - OWN), F32)], axis=1)
    listed = jnp.concatenate([listed, jnp.zeros((BLK - SLOTS, BLK), F32)], axis=0).T
    copies = []
    for k, out in ((1, upper), (0, lower)):
        tiles = []
        for t in range(HALF * k, HALF * k + HALF):
            rows = jnp.concatenate(
                [
                    positions[:, t * BLK : (t + 1) * BLK],
                    radius[t : t + 1],
                    listed[t : t + 1],
                    jnp.zeros((3, BLK), F32),
                ],
                axis=0,
            )
            geo[t] = rows
            tiles.append(rows)
        rest = jnp.concatenate(tiles, axis=0)
        for part in range(3):
            coarse = rest.astype(BF16)
            rest = rest - coarse.astype(F32)
            ext[k, :, part * BLK : (part + 1) * BLK] = coarse
        copies.append(
            pltpu.make_async_copy(ext.at[k], out.at[:, pl.ds(width, WIDTH)], sems.at[6 + k])
        )
        copies[-1].start()
    for k, out in ((1, upper), (0, lower)):
        halves[k].wait()
        copies.append(
            pltpu.make_async_copy(
                panel.at[:, pl.ds(width * k, width)], out.at[:, pl.ds(0, width)], sems.at[8 + k]
            )
        )
        copies[-1].start()
    for copy in copies:
        copy.wait()


def own_kernel(
    row, panel, geo, gain, out, scaled, geo_col, left, right, pairs, near, near_all, acc, mat_a, mat_b, sem
):
    near_all[...] = geo[:, 4, :].astype(jnp.int32)
    fetch = pltpu.make_async_copy(near_all, near, sem.at[0])
    fetch.start()
    acc[...] = jnp.zeros_like(acc)
    fetch.wait()
    first = row[0] * OWN

    def step(index, count):
        for k in range(3):
            t = 3 * index + k
            parts = split(panel, t)
            turn_parts(t, parts, left)
            parts = [(part.astype(F32) * gain[...]).astype(BF16) for part in parts]
            turn_parts(t, parts, scaled)
            for c in range(3):
                right[t, c] = parts[c]
            columns = turned_geo(geo[t])
            for c in range(4):
                geo_col[t, c] = jnp.broadcast_to(columns[:, c : c + 1], (BLK, BLK))
            for slot in range(SLOTS):
                j = near[t, slot] - first
                pairs[count] = encode(t, 0, t, 0) + j
                count = count + ((j >= 0) & (j < OWN)).astype(jnp.int32)
        return count

    def todo_of(n):
        code = pairs[n]
        dest = code >> 15
        return dest, 0, jnp.minimum(dest, OWN - 1), (code & 511) - 16 * jnp.minimum(dest, OWN - 1)

    count = lax.fori_loop(0, OWN // 3, step, jnp.int32(0))
    for k in range(UNROLL):
        pairs[count + k] = encode(OWN, 0, OWN - 1, 0)
    steps(count, todo_of, left, right, geo, geo_col, (mat_a, mat_b), acc)
    out[...] = acc[pl.ds(0, OWN)]


def side_kernel(high, row, start, scaled, geo_col, message, geo, out, *scratch):
    pairs, near, near_all, acc, halo_row, turn_a, turn_b, mat_a, mat_b, sem = scratch
    width = HALF * WIDTH
    rows = [message[:, width + k * BLK : width + (k + 1) * BLK].astype(F32) for k in range(3)]
    halo = (rows[0] + rows[1] + rows[2]).reshape(HALF, 8, BLK)
    near_all[pl.ds(0, OWN)] = geo[:, 4, :].astype(jnp.int32)
    near_all[pl.ds(OWN, 16)] = jnp.concatenate(
        [halo[:, 4, :].astype(jnp.int32), jnp.zeros((4, BLK), jnp.int32)], axis=0
    )
    fetch = pltpu.make_async_copy(near_all, near, sem.at[0])
    fetch.start()
    halo_row[...] = halo
    if high:
        acc[...] = start[...]
    else:
        acc[pl.ds(0, OWN)] = start[...]
        acc[pl.ds(OWN, OWN + 1)] = jnp.zeros((OWN + 1, 3, 8, BLK), F32)

    r = row[0]
    first = r * OWN
    base = 0 if high else HALF
    exists = (r < 15) if high else (r > 0)

    def facing(n):
        n = jnp.minimum(n, HALF - 1)
        return OWN + base + n, base + n, n, base + n

    def scan(step, count):
        for slot in range(2, SLOTS):
            for k in range(4):
                h = 4 * step + k
                i = near[OWN + h, slot] - first
                pairs[count] = encode(OWN + base + h, TRASH, i, h)
                keep = exists & (i >= base) & (i < OWN)
                count = count + keep.astype(jnp.int32)
                for t in (h, HALF + h) if high else (HALF + h,):
                    j = near[t, slot] - first - (OWN if high else -HALF)
                    pairs[count] = encode(TRASH, t, t, j)
                    count = count + ((j >= 0) & (j < HALF)).astype(jnp.int32)
        return count

    fetch.wait()
    rest = (scaled, Columns(message), halo_row, geo_col, (mat_a, mat_b), acc, (turn_a, turn_b))
    count = steps(HALF, facing, *rest, before=scan)
    for k in range(UNROLL):
        pairs[count + k] = encode(TRASH, TRASH, 0, 0)
    steps(count, lambda n: decode(pairs[n]), *rest)
    if not high:
        out[...] = acc[...]
        return
    for m in range(OWN // 3):
        for part in range(2):
            tiles = []
            for t in range(3 * m, 3 * m + 3):
                tiles.append(-3.0 * jnp.sum(acc[OWN * part + t], axis=1))
            line = jnp.concatenate(tiles, axis=1)
            half = 3 * BLK // 2
            out[2 * m, pl.ds(3 * part, 3)] = line[:, :half]
            out[2 * m + 1, pl.ds(3 * part, 3)] = line[:, half:]


VMEM = pl.BlockSpec(memory_space=pltpu.VMEM)
SMEM = pl.BlockSpec(memory_space=pltpu.SMEM)
ANY = pl.BlockSpec(memory_space=pl.ANY)


def stacks(tiles):
    return (tiles, 3, BLK, 2 * DEPTH), (tiles, 3, DEPTH, BLK)


def cost(pairs):
    return pl.CostEstimate(
        flops=pairs * 2 * 3 * BLK * 2 * BLK * 2 * DEPTH, bytes_accessed=8 << 20, transcendentals=0
    )


def own_call(row, panel, geo, gain):
    left, right = stacks(OWN)
    return pl.pallas_call(
        own_kernel,
        out_shape=(
            jax.ShapeDtypeStruct((OWN, 3, 8, BLK), F32),
            jax.ShapeDtypeStruct(left, BF16),
            jax.ShapeDtypeStruct((OWN, 4, BLK, BLK), F32),
        ),
        in_specs=[SMEM, VMEM, VMEM, VMEM],
        out_specs=(VMEM, VMEM, VMEM),
        scratch_shapes=[
            pltpu.VMEM(left, BF16),
            pltpu.VMEM(right, BF16),
            pltpu.SMEM((OWN * SLOTS + UNROLL + 4,), jnp.int32),
            pltpu.SMEM((OWN, BLK), jnp.int32),
            pltpu.VMEM((OWN, BLK), jnp.int32),
            pltpu.VMEM((OWN + 1, 3, 8, BLK), F32),
            pltpu.VMEM((6, BLK, BLK), F32),
            pltpu.VMEM((6, BLK, BLK), F32),
            pltpu.SemaphoreType.DMA((1,)),
        ],
        compiler_params=pltpu.CompilerParams(vmem_limit_bytes=20 << 20),
        cost_estimate=cost(40),
        name="own_pairs",
    )(row, panel, geo, gain)


def side_call(high, *args):
    if high:
        shape = jax.ShapeDtypeStruct((2 * OWN // 3, 6, 3 * BLK // 2), F32)
    else:
        shape = jax.ShapeDtypeStruct((TRASH + 1, 3, 8, BLK), F32)
    return pl.pallas_call(
        functools.partial(side_kernel, high),
        out_shape=shape,
        in_specs=[SMEM] + [VMEM] * 5,
        out_specs=VMEM,
        scratch_shapes=[
            pltpu.SMEM((3 * HALF * (SLOTS - 2) + UNROLL + 4,), jnp.int32),
            pltpu.SMEM((OWN + 16, BLK), jnp.int32),
            pltpu.VMEM((OWN + 16, BLK), jnp.int32),
            pltpu.VMEM((TRASH + 1, 3, 8, BLK), F32),
            pltpu.VMEM((HALF, 8, BLK), F32),
            pltpu.VMEM((3, BLK, BLK), F32),
            pltpu.VMEM((3, BLK, BLK), F32),
            pltpu.VMEM((6, BLK, BLK), F32),
            pltpu.VMEM((6, BLK, BLK), F32),
            pltpu.SemaphoreType.DMA((1,)),
        ],
        compiler_params=pltpu.CompilerParams(vmem_limit_bytes=20 << 20),
        cost_estimate=cost(30),
        name="above_pairs" if high else "below_pairs",
    )(*args)


def pack_call(panel, positions, elements, radii, nbr):
    message = jax.ShapeDtypeStruct((DEPTH, (HALF + 1) * WIDTH), BF16)
    return pl.pallas_call(
        pack_kernel,
        out_shape=(jax.ShapeDtypeStruct((OWN, 8, BLK), F32), message, message),
        in_specs=[ANY] * 5,
        out_specs=(VMEM, ANY, ANY),
        scratch_shapes=[
            pltpu.VMEM(panel.shape, BF16),
            pltpu.VMEM((2, DEPTH, WIDTH), BF16),
            pltpu.VMEM(positions.shape, F32),
            pltpu.VMEM(elements.shape, jnp.int32),
            pltpu.VMEM(radii.shape, F32),
            pltpu.VMEM(nbr.shape, jnp.int32),
            pltpu.SemaphoreType.DMA((10,)),
        ],
        compiler_params=pltpu.CompilerParams(vmem_limit_bytes=56 << 20),
        name="pack",
    )(panel, positions, elements, radii, nbr)


def per_device(panel, eigenvalues, positions, elements, radii, neighbors):
    rows = lax.axis_size("row")
    up = [(k, k + 1) for k in range(rows - 1)]
    down = [(k + 1, k) for k in range(rows - 1)]
    geo, lower, upper = pack_call(
        panel, positions, elements.reshape(OWN, BLK), radii[None], neighbors.T
    )
    lo = lax.ppermute(upper, "row", up)
    hi = lax.ppermute(lower, "row", down)

    gain = jnp.broadcast_to((0.25 / jnp.sqrt(eigenvalues))[:, None], (DEPTH, BLK))
    row = lax.axis_index("row").astype(jnp.int32).reshape(1)
    start, *own = own_call(row, panel, geo, gain)
    start = side_call(False, row, start, *own, lo, geo)
    forces = side_call(True, row, start, *own, hi, geo)

    cols = lax.axis_size("col")
    part = jnp.sum(lax.all_to_all(forces, "col", 0, 0, tiled=True), axis=0)
    back = []
    for k in range(rows):
        for c in range(cols):
            to = k + 1 if c < cols // 2 else k - 1
            if 0 <= to < rows:
                back.append((k * cols + c, to * cols + c))
    return part[:3] + lax.ppermute(part[3:], ("row", "col"), back)


def solution(mesh):
    return jax.shard_map(
        per_device,
        mesh=mesh,
        in_specs=(P("col", "row"), P("col"), P(None, "row"), P("row"), P(), P("row", None)),
        out_specs=P(None, ("row", "col")),
        check_vma=False,
    )
```

```python
import functools

import jax
import jax.numpy as jnp
from jax import lax
from jax.experimental import pallas as pl
from jax.experimental.pallas import tpu as pltpu
from jax.sharding import PartitionSpec as P

BLK = 128
OWN = 24
HALF = 12
TRASH = 2 * OWN
LOCAL = OWN + 2 * HALF
SLOTS = 5
DEPTH = 96
WIDTH = 3 * BLK
UNROLL = 6
F32 = jnp.float32
BF16 = jnp.bfloat16


def products(i, j, left, right, out):
    zero = jnp.zeros((DEPTH, BLK), BF16)
    for slot, (a, b, first) in enumerate(((0, 1, True), (0, 2, False), (1, 2, True))):
        col_a, col_b = right[i, a], right[i, b]
        if first:
            diag = jnp.concatenate([col_a * BF16(2), zero], axis=0)
        else:
            diag = jnp.concatenate([zero, col_b * BF16(2)], axis=0)
        rhs = jnp.concatenate([jnp.concatenate([col_b, col_a], axis=0), diag], axis=1)
        res = lax.dot_general(
            left[j, slot], rhs, (((1,), (0,)), ((), ())), preferred_element_type=F32
        )
        out[2 * slot] = res[:, :BLK]
        out[2 * slot + 1] = res[:, BLK:]


def contract(dest, i, j, mats, geo_row, geo_col, acc, back=None, turned=None):
    own = [jnp.broadcast_to(geo_row[i, c : c + 1, :], (8, BLK)) for c in range(4)]
    total = [None, None, None]
    for strip in range(BLK // 8):
        at = pl.ds(8 * strip, 8)
        other = [geo_col[j, c, at, :] for c in range(4)]
        d = [own[c] - other[c] for c in range(3)]
        s = own[3] + other[3]
        m01, m00, m02, m22, m12, m11 = (mats[k, at, :] for k in range(6))
        u = (d[0] * d[0] + d[1] * d[1]) + (d[2] * d[2] + s * s)
        y = lax.rsqrt(u)
        y2 = y * y
        f5 = y2 * y2 * y
        v0 = m00 * d[0] + m01 * d[1] + m02 * d[2]
        v1 = m01 * d[0] + m11 * d[1] + m12 * d[2]
        v2 = m02 * d[0] + m12 * d[1] + m22 * d[2]
        q = d[0] * v0 + d[1] * v1 + d[2] * v2
        w = (m00 + m11 + m22) * 0.5 - (y2 * 2.5) * q
        terms = [f5 * (v + d[c] * w) for c, v in enumerate((v0, v1, v2))]
        for c, term in enumerate(terms):
            total[c] = term if total[c] is None else total[c] + term
        if turned is not None:
            for c, term in enumerate(terms):
                turned[c, at, :] = term
    for c in range(3):
        acc[dest, c] = acc[dest, c] + total[c]
    if turned is not None:
        for c in range(3):
            flipped = jnp.sum(turned[c].T.reshape(BLK // 8, 8, BLK), axis=0)
            acc[back, c] = acc[back, c] - flipped


def split(src, first):
    at = pl.multiple_of(first * WIDTH, BLK)
    return [src[:, pl.ds(at + c * BLK, BLK)] for c in range(3)]


def turn_parts(tile, parts, left):
    for slot, (a, b) in enumerate(((0, 1), (0, 2), (1, 2))):
        left[tile, slot] = jnp.concatenate([parts[a], parts[b]], axis=0).T


def turned_geo(rows):
    return jnp.concatenate([rows, jnp.zeros((BLK - 8, BLK), F32)], axis=0).T


def encode(dest, back, own, halo):
    return dest * 32768 + back * 512 + own * 16 + halo


def decode(code):
    return code >> 15, (code >> 9) & 63, code & 15, (code >> 4) & 31


class Columns:
    def __init__(self, ref):
        self.ref = ref

    def __getitem__(self, at):
        tile, c = at
        return self.ref[:, pl.ds(pl.multiple_of(tile * WIDTH + c * BLK, BLK), BLK)]


def steps(count, todo_of, left, right, geo_row, geo_col, mats, acc, turned=None, before=None):
    _, _, i, j = todo_of(jnp.int32(0))
    products(i, j, left, right, mats[0])

    def body(step, carry):
        if before is not None:
            carry = before(step, carry)
        todo = [todo_of(step * UNROLL + k) for k in range(UNROLL + 1)]
        for k in range(UNROLL):
            products(todo[k + 1][2], todo[k + 1][3], left, right, mats[(k + 1) % 2])
            dest, back, i, j = todo[k]
            turn = None if turned is None else turned[k % 2]
            contract(dest, i, j, mats[k % 2], geo_row, geo_col, acc, back, turn)
        return carry

    return lax.fori_loop(0, (count + UNROLL - 1) // UNROLL, body, jnp.int32(0))


def pack_kernel(
    panel_hbm, positions_hbm, elements_hbm, radii_hbm, nbr_hbm, geo, lower, upper,
    panel, ext, positions, elements, radii, nbr, sems,
):
    width = HALF * WIDTH
    small = [
        pltpu.make_async_copy(src, dst, sems.at[k])
        for k, (src, dst) in enumerate(
            ((positions_hbm, positions), (elements_hbm, elements), (radii_hbm, radii), (nbr_hbm, nbr))
        )
    ]
    halves = [
        pltpu.make_async_copy(
            panel_hbm.at[:, pl.ds(width * k, width)], panel.at[:, pl.ds(width * k, width)], sems.at[4 + k]
        )
        for k in range(2)
    ]
    for copy in small + [halves[1], halves[0]]:
        copy.start()
    for copy in small:
        copy.wait()
    kinds = elements[...]
    radius = jnp.zeros((OWN, BLK), F32)
    for kind in range(radii.shape[1]):
        radius = jnp.where(kinds == kind, radii[0:1, kind : kind + 1], radius)
    listed = nbr[...].astype(F32)
    listed = jnp.concatenate([listed, jnp.zeros((SLOTS, BLK - OWN), F32)], axis=1)
    listed = jnp.concatenate([listed, jnp.zeros((BLK - SLOTS, BLK), F32)], axis=0).T
    copies = []
    for k, out in ((1, upper), (0, lower)):
        tiles = []
        for t in range(HALF * k, HALF * k + HALF):
            rows = jnp.concatenate(
                [
                    positions[:, t * BLK : (t + 1) * BLK],
                    radius[t : t + 1],
                    listed[t : t + 1],
                    jnp.zeros((3, BLK), F32),
                ],
                axis=0,
            )
            geo[t] = rows
            tiles.append(rows)
        rest = jnp.concatenate(tiles, axis=0)
        for part in range(3):
            coarse = rest.astype(BF16)
            rest = rest - coarse.astype(F32)
            ext[k, :, part * BLK : (part + 1) * BLK] = coarse
        copies.append(
            pltpu.make_async_copy(ext.at[k], out.at[:, pl.ds(width, WIDTH)], sems.at[6 + k])
        )
        copies[-1].start()
    for k, out in ((1, upper), (0, lower)):
        halves[k].wait()
        copies.append(
            pltpu.make_async_copy(
                panel.at[:, pl.ds(width * k, width)], out.at[:, pl.ds(0, width)], sems.at[8 + k]
            )
        )
        copies[-1].start()
    for copy in copies:
        copy.wait()


def own_kernel(
    row, panel, geo, gain, out, scaled, geo_col, left, right, pairs, near, near_all, acc, mat_a, mat_b, sem
):
    near_all[...] = geo[:, 4, :].astype(jnp.int32)
    fetch = pltpu.make_async_copy(near_all, near, sem.at[0])
    fetch.start()
    acc[...] = jnp.zeros_like(acc)
    fetch.wait()
    first = row[0] * OWN

    def step(index, count):
        for k in range(3):
            t = 3 * index + k
            parts = split(panel, t)
            turn_parts(t, parts, left)
            parts = [(part.astype(F32) * gain[...]).astype(BF16) for part in parts]
            turn_parts(t, parts, scaled)
            for c in range(3):
                right[t, c] = parts[c]
            columns = turned_geo(geo[t])
            for c in range(4):
                geo_col[t, c] = jnp.broadcast_to(columns[:, c : c + 1], (BLK, BLK))
            for slot in range(SLOTS):
                j = near[t, slot] - first
                pairs[count] = encode(t, 0, t, 0) + j
                count = count + ((j >= 0) & (j < OWN)).astype(jnp.int32)
        return count

    def todo_of(n):
        code = pairs[n]
        dest = code >> 15
        return dest, 0, jnp.minimum(dest, OWN - 1), (code & 511) - 16 * jnp.minimum(dest, OWN - 1)

    count = lax.fori_loop(0, OWN // 3, step, jnp.int32(0))
    for k in range(UNROLL):
        pairs[count + k] = encode(OWN, 0, OWN - 1, 0)
    steps(count, todo_of, left, right, geo, geo_col, (mat_a, mat_b), acc)
    out[...] = acc[pl.ds(0, OWN)]


def side_kernel(high, row, start, scaled, geo_col, message, geo, out, *scratch):
    pairs, near, near_all, acc, halo_row, turn_a, turn_b, mat_a, mat_b, sem = scratch
    width = HALF * WIDTH
    rows = [message[:, width + k * BLK : width + (k + 1) * BLK].astype(F32) for k in range(3)]
    halo = (rows[0] + rows[1] + rows[2]).reshape(HALF, 8, BLK)
    near_all[pl.ds(0, OWN)] = geo[:, 4, :].astype(jnp.int32)
    near_all[pl.ds(OWN, 16)] = jnp.concatenate(
        [halo[:, 4, :].astype(jnp.int32), jnp.zeros((4, BLK), jnp.int32)], axis=0
    )
    fetch = pltpu.make_async_copy(near_all, near, sem.at[0])
    fetch.start()
    halo_row[...] = halo
    if high:
        acc[...] = start[...]
    else:
        acc[pl.ds(0, OWN)] = start[...]
        acc[pl.ds(OWN, OWN + 1)] = jnp.zeros((OWN + 1, 3, 8, BLK), F32)

    r = row[0]
    first = r * OWN
    base = 0 if high else HALF
    exists = (r < 15) if high else (r > 0)

    def facing(n):
        n = jnp.minimum(n, HALF - 1)
        return OWN + base + n, base + n, n, base + n

    def scan(step, count):
        for slot in range(2, SLOTS):
            for k in range(UNROLL):
                h = UNROLL * step + k
                i = near[OWN + h, slot] - first
                pairs[count] = encode(OWN + base + h, TRASH, i, h)
                keep = exists & (i >= base) & (i < OWN)
                count = count + keep.astype(jnp.int32)
                for t in (h, HALF + h) if high else (HALF + h,):
                    j = near[t, slot] - first - (OWN if high else -HALF)
                    pairs[count] = encode(TRASH, t, t, j)
                    count = count + ((j >= 0) & (j < HALF)).astype(jnp.int32)
        return count

    fetch.wait()
    rest = (scaled, Columns(message), halo_row, geo_col, (mat_a, mat_b), acc, (turn_a, turn_b))
    count = steps(HALF, facing, *rest, before=scan)
    for k in range(UNROLL):
        pairs[count + k] = encode(TRASH, TRASH, 0, 0)
    steps(count, lambda n: decode(pairs[n]), *rest)
    if not high:
        out[...] = acc[...]
        return
    for m in range(OWN // 3):
        for part in range(2):
            tiles = []
            for t in range(3 * m, 3 * m + 3):
                tiles.append(-3.0 * jnp.sum(acc[OWN * part + t], axis=1))
            line = jnp.concatenate(tiles, axis=1)
            half = 3 * BLK // 2
            out[2 * m, pl.ds(3 * part, 3)] = line[:, :half]
            out[2 * m + 1, pl.ds(3 * part, 3)] = line[:, half:]


VMEM = pl.BlockSpec(memory_space=pltpu.VMEM)
SMEM = pl.BlockSpec(memory_space=pltpu.SMEM)
ANY = pl.BlockSpec(memory_space=pl.ANY)


def stacks(tiles):
    return (tiles, 3, BLK, 2 * DEPTH), (tiles, 3, DEPTH, BLK)


def cost(pairs):
    return pl.CostEstimate(
        flops=pairs * 2 * 3 * BLK * 2 * BLK * 2 * DEPTH, bytes_accessed=8 << 20, transcendentals=0
    )


def own_call(row, panel, geo, gain):
    left, right = stacks(OWN)
    return pl.pallas_call(
        own_kernel,
        out_shape=(
            jax.ShapeDtypeStruct((OWN, 3, 8, BLK), F32),
            jax.ShapeDtypeStruct(left, BF16),
            jax.ShapeDtypeStruct((OWN, 4, BLK, BLK), F32),
        ),
        in_specs=[SMEM, VMEM, VMEM, VMEM],
        out_specs=(VMEM, VMEM, VMEM),
        scratch_shapes=[
            pltpu.VMEM(left, BF16),
            pltpu.VMEM(right, BF16),
            pltpu.SMEM((OWN * SLOTS + UNROLL + 4,), jnp.int32),
            pltpu.SMEM((OWN, BLK), jnp.int32),
            pltpu.VMEM((OWN, BLK), jnp.int32),
            pltpu.VMEM((OWN + 1, 3, 8, BLK), F32),
            pltpu.VMEM((6, BLK, BLK), F32),
            pltpu.VMEM((6, BLK, BLK), F32),
            pltpu.SemaphoreType.DMA((1,)),
        ],
        compiler_params=pltpu.CompilerParams(vmem_limit_bytes=20 << 20),
        cost_estimate=cost(40),
        name="own_pairs",
    )(row, panel, geo, gain)


def side_call(high, *args):
    if high:
        shape = jax.ShapeDtypeStruct((2 * OWN // 3, 6, 3 * BLK // 2), F32)
    else:
        shape = jax.ShapeDtypeStruct((TRASH + 1, 3, 8, BLK), F32)
    return pl.pallas_call(
        functools.partial(side_kernel, high),
        out_shape=shape,
        in_specs=[SMEM] + [VMEM] * 5,
        out_specs=VMEM,
        scratch_shapes=[
            pltpu.SMEM((3 * HALF * (SLOTS - 2) + UNROLL + 4,), jnp.int32),
            pltpu.SMEM((OWN + 16, BLK), jnp.int32),
            pltpu.VMEM((OWN + 16, BLK), jnp.int32),
            pltpu.VMEM((TRASH + 1, 3, 8, BLK), F32),
            pltpu.VMEM((HALF, 8, BLK), F32),
            pltpu.VMEM((3, BLK, BLK), F32),
            pltpu.VMEM((3, BLK, BLK), F32),
            pltpu.VMEM((6, BLK, BLK), F32),
            pltpu.VMEM((6, BLK, BLK), F32),
            pltpu.SemaphoreType.DMA((1,)),
        ],
        compiler_params=pltpu.CompilerParams(vmem_limit_bytes=20 << 20),
        cost_estimate=cost(30),
        name="above_pairs" if high else "below_pairs",
    )(*args)


def pack_call(panel, positions, elements, radii, nbr):
    message = jax.ShapeDtypeStruct((DEPTH, (HALF + 1) * WIDTH), BF16)
    return pl.pallas_call(
        pack_kernel,
        out_shape=(jax.ShapeDtypeStruct((OWN, 8, BLK), F32), message, message),
        in_specs=[ANY] * 5,
        out_specs=(VMEM, ANY, ANY),
        scratch_shapes=[
            pltpu.VMEM(panel.shape, BF16),
            pltpu.VMEM((2, DEPTH, WIDTH), BF16),
            pltpu.VMEM(positions.shape, F32),
            pltpu.VMEM(elements.shape, jnp.int32),
            pltpu.VMEM(radii.shape, F32),
            pltpu.VMEM(nbr.shape, jnp.int32),
            pltpu.SemaphoreType.DMA((10,)),
        ],
        compiler_params=pltpu.CompilerParams(vmem_limit_bytes=56 << 20),
        name="pack",
    )(panel, positions, elements, radii, nbr)


def per_device(panel, eigenvalues, positions, elements, radii, neighbors):
    rows = lax.axis_size("row")
    up = [(k, k + 1) for k in range(rows - 1)]
    down = [(k + 1, k) for k in range(rows - 1)]
    geo, lower, upper = pack_call(
        panel, positions, elements.reshape(OWN, BLK), radii[None], neighbors.T
    )
    lo = lax.ppermute(upper, "row", up)
    hi = lax.ppermute(lower, "row", down)

    gain = jnp.broadcast_to((0.25 / jnp.sqrt(eigenvalues))[:, None], (DEPTH, BLK))
    row = lax.axis_index("row").astype(jnp.int32).reshape(1)
    start, *own = own_call(row, panel, geo, gain)
    start = side_call(False, row, start, *own, lo, geo)
    forces = side_call(True, row, start, *own, hi, geo)

    cols = lax.axis_size("col")
    part = jnp.sum(lax.all_to_all(forces, "col", 0, 0, tiled=True), axis=0)
    back = []
    for k in range(rows):
        for c in range(cols):
            to = k + 1 if c < cols // 2 else k - 1
            if 0 <= to < rows:
                back.append((k * cols + c, to * cols + c))
    return part[:3] + lax.ppermute(part[3:], ("row", "col"), back)


def solution(mesh):
    return jax.shard_map(
        per_device,
        mesh=mesh,
        in_specs=(P("col", "row"), P("col"), P(None, "row"), P("row"), P(), P("row", None)),
        out_specs=P(None, ("row", "col")),
        check_vma=False,
    )
```
